512 devices in a mesh: row: 16 (over y, core), col: 32 (over z, x).
Axes of the slice: x: 4, y: 8, z: 8, core: 2. Of those that a mesh axis runs over, the one named last changes fastest.
Arguments:
- patches: float32 [512, 6144], P('col', 'row'), may hold values from -6 to 6
- cotangent: float32 [512, 6144], P('col', 'row'), may hold values from -1.5 to 1.5
- expand_weight: float32 [6144, 12288], P('row', 'col'), may hold values from -0.078125 to 0.078125
- reduce_weight: float32 [12288, 6144], P('col', 'row'), may hold values from -0.0546875 to 0.0546875
Outputs:
- mlp_output: float32 [512, 6144], P('col', 'row')
- patch_grad: float32 [512, 6144], P('col', 'row')
- expand_grad: float32 [6144, 12288], P('row', 'col')
- reduce_grad: float32 [12288, 6144], P('col', 'row')
The draws below stay inside these ranges and needn't reach their ends.
All inputs are finite; a program needn't handle non-finite values.
Results may differ from the reference program's by a relative error of at most 0.00012.
Values sent between devices are 32-bit elements; how exact they have to be, the bound alone decides.
No kernel may reach another device: no remote copies, remote signals or barrier semaphores. Data moves between devices by JAX's collectives and lax.ppermute only.
A program may use at most 64 MiB of HBM per device.

```python
import math
import jax
import jax.numpy as jnp
from jax import lax

D = 6144
FF = 12288
TOKENS = 512


def level_of(stream_key, extent, pieces, least, largest):
    gain, own = 1.0, jax.random.fold_in(stream_key, 6)
    for position, parts in pieces:
        draws = jnp.exp(jax.random.uniform(jax.random.fold_in(own, position), (parts,), jnp.float32, least / len(pieces), largest / len(pieces)))
        gain = gain * jnp.repeat(draws, extent[position] // parts).reshape([-1 if axis == position else 1 for axis in range(len(extent))])
    return gain


def noise(stream_key, dims, spread, reach, cuts=(), held_as=jnp.bfloat16):
    drawn = jax.random.normal(stream_key, dims, jnp.float32) * spread
    if len(cuts) > 0:
        drawn = level_of(stream_key, dims, cuts, -0.22, 0.18) * drawn
    return jnp.clip(drawn, min=-reach, max=reach).astype(held_as)


def setup_inputs(seed: int = 0) -> dict:
    key_list = jax.random.split(jax.random.key(seed), 5)
    patches = noise(key_list[0], (TOKENS, D), 1.0, 6.0, ((0, 32), (1, 16)), jnp.float32)
    cotangent = noise(key_list[1], (TOKENS, D), 0.25, 1.5, ((0, 32), (1, 16)), jnp.float32)
    expand_weight = noise(key_list[2], (D, FF), D ** -0.5, 0.078125, ((0, 16), (1, 32)), jnp.float32)
    reduce_weight = noise(key_list[3], (FF, D), FF ** -0.5, 0.0546875, ((0, 32), (1, 16)), jnp.float32)
    return {"patches": patches, "cotangent": cotangent, "expand_weight": expand_weight, "reduce_weight": reduce_weight}


highest = lax.Precision.HIGHEST

def matmul(left, right):
    return jnp.dot(left, right, precision=highest, preferred_element_type=jnp.float32)

def reference(patches, cotangent, expand_weight, reduce_weight):
    preact = matmul(patches, expand_weight)
    act_cdf = 0.5 * (1.0 + jax.scipy.special.erf(preact / math.sqrt(2.0)))
    activated = preact * act_cdf
    mlp_output = matmul(activated, reduce_weight)
    act_grad = matmul(cotangent, reduce_weight.T)
    pre_grad = act_grad * (act_cdf + preact * jnp.exp(-0.5 * preact * preact) / math.sqrt(2.0 * math.pi))
    patch_grad = matmul(pre_grad, expand_weight.T)
    expand_grad = matmul(patches.T, pre_grad)
    reduce_grad = matmul(activated.T, cotangent)
    return (mlp_output, patch_grad, expand_grad, reduce_grad)
```

```python
import math

import jax
import jax.numpy as jnp
from jax import lax
from jax.sharding import Mesh, PartitionSpec as P

precise = lax.Precision.HIGH
Y, CORE, Z, X = 8, 2, 8, 4


def product(left, right, dims):
    return lax.dot_general(
        left, right, (dims, ((), ())), precision=precise, preferred_element_type=jnp.float32
    )


def from_x(block, step):
    return lax.ppermute(block, "x", [((i + step) % X, i) for i in range(X)])


def to_x(block, step):
    return lax.ppermute(block, "x", [(i, (i + step) % X) for i in range(X)])


def swap_cores(block):
    return lax.ppermute(block, "core", [(0, 1), (1, 0)])


def everyone(block, axis, size):
    copies = jnp.broadcast_to(block[None], (size, *block.shape))
    return lax.all_to_all(copies, axis, split_axis=0, concat_axis=0, tiled=True)


def own_half_first(block, core):
    half = block.shape[0] // 2
    first, second = block[:half], block[half:]
    return jnp.stack(
        [jnp.where(core == 0, first, second), jnp.where(core == 0, second, first)]
    )


def shards(patches, cotangent, expand_weight, reduce_weight):
    core = lax.axis_index("core")
    width = patches.shape[1]
    hidden = expand_weight.shape[1]
    tokens = patches.shape[0]
    half = tokens // 2

    mine = own_half_first(jnp.concatenate([patches, cotangent], axis=1), core)
    over_z = everyone(mine, "z", Z)
    over_z = over_z.transpose(1, 0, 2, 3).reshape(2, Z * half, 2 * width)
    pieces = [over_z] + [from_x(over_z, k) for k in (1, 2, 3)]
    gathered = jnp.stack(pieces, axis=1)
    gathered = gathered.reshape(2, X * Z * half, 2 * width)
    full_in, full_cot = gathered[..., :width], gathered[..., width:]

    def terms(part):
        return jnp.concatenate(
            [
                product(full_in[part], expand_weight, ((1,), (0,))),
                product(full_cot[part], reduce_weight, ((1,), (1,))),
            ],
            axis=1,
        )

    away = swap_cores(terms(1))
    summed = terms(0) + away
    share = summed.shape[0] // Y
    parts = lax.all_to_all(
        summed.reshape(Y, share, 2 * hidden), "y", split_axis=0, concat_axis=0, tiled=True
    )
    total = jnp.sum(parts, axis=0)
    preact, act_grad = total[:, :hidden], total[:, hidden:]
    act_cdf = 0.5 * (1.0 + jax.scipy.special.erf(preact / math.sqrt(2.0)))
    activated = preact * act_cdf
    pre_grad = act_grad * (
        act_cdf + preact * jnp.exp(-0.5 * preact * preact) / math.sqrt(2.0 * math.pi)
    )
    near = everyone(jnp.concatenate([activated, pre_grad], axis=1), "y", Y)
    near = near.reshape(Y * share, 2 * hidden)
    far = swap_cores(near)
    both = jnp.stack([near, far])

    def results(part):
        return jnp.concatenate(
            [
                product(part[:, :hidden], reduce_weight, ((1,), (0,))),
                product(part[:, hidden:], expand_weight, ((1,), (1,))),
            ],
            axis=1,
        )

    outs = jnp.stack([results(near), results(far)]).reshape(2, X, Z, half, 2 * width)
    outs = outs.transpose(1, 2, 0, 3, 4)
    summed = outs[0]
    arrived = [to_x(outs[k], k) for k in (1, 2, 3)]
    summed = summed + arrived[0] + arrived[1] + arrived[2]
    last = jnp.sum(
        lax.all_to_all(summed, "z", split_axis=0, concat_axis=0, tiled=True), axis=0
    )
    last = own_half_first(last.reshape(tokens, 2 * width), core).reshape(tokens, 2 * width)

    flat = both.reshape(-1, 2 * hidden)
    all_in = full_in.reshape(-1, width)
    all_cot = full_cot.reshape(-1, width)
    expand_grad = product(all_in, flat[:, hidden:], ((0,), (0,)))
    reduce_grad = product(flat[:, :hidden], all_cot, ((0,), (0,)))
    return last[:, :width], last[:, width:], expand_grad, reduce_grad


def solution(mesh):
    fine = Mesh(mesh.devices.reshape(Y, CORE, Z, X), ("y", "core", "z", "x"))
    row, col = ("y", "core"), ("z", "x")
    placed = (P(col, row), P(col, row), P(row, col), P(col, row))
    return jax.shard_map(
        shards, mesh=fine, in_specs=placed, out_specs=placed, check_vma=False
    )
```

```python
import math

import jax
import jax.numpy as jnp
from jax import lax
from jax.sharding import Mesh, PartitionSpec as P

precise = lax.Precision.HIGH
Y, CORE, ZH, ZL, XH, XL = 8, 2, 4, 2, 2, 2
N_FAR, N_NEAR = ZH * XH, ZL * XL
Z, X = ZH * ZL, XH * XL
FAR = ("zh", "xh", "core")
CELL = ("core", "zh", "zl", "xh", "xl")
BLOCKS = [
    [
        (c * Z + (z + (p + c) % 2 + c) % Z) * X + (x + (q + c) % 2 + c) % X
        for p in range(2)
        for q in range(2)
    ]
    for c in range(CORE)
    for z in range(0, Z, 2)
    for x in range(0, X, 2)
]


def product(left, right, dims):
    return lax.dot_general(
        left, right, (dims, ((), ())), precision=precise, preferred_element_type=jnp.float32
    )


def swap_cores(block):
    return lax.ppermute(block, "core", [(0, 1), (1, 0)])


def exchange(blocks, axis, groups=None):
    return lax.all_to_all(
        blocks, axis, split_axis=0, concat_axis=0, tiled=True, axis_index_groups=groups
    )


def copies(block, count):
    return jnp.broadcast_to(block[None], (count, *block.shape))


def shards(patches, cotangent, expand_weight, reduce_weight):
    core = lax.axis_index("core")
    tokens, width = patches.shape
    hidden = expand_weight.shape[1]
    part = tokens // CORE

    def in_order(own, other):
        return jnp.where(core == 0, own, other), jnp.where(core == 0, other, own)

    mine = jnp.stack(
        [patches.reshape(CORE, part, width), cotangent.reshape(CORE, part, width)], axis=1
    )
    far = exchange(copies(mine, N_FAR).reshape(N_FAR * CORE, 2, part, width), FAR)
    far = far.reshape(N_FAR, CORE, 2, part, width).transpose(1, 2, 0, 3, 4)
    far = far.reshape(CORE, 2, N_FAR * part, width)
    inputs = exchange(copies(far, N_NEAR), CELL, BLOCKS)
    rows = N_NEAR * N_FAR * part

    others = swap_cores(jnp.stack([expand_weight, reduce_weight]))
    expand = in_order(expand_weight, others[0])
    reduce = in_order(reduce_weight, others[1])

    full_in = [inputs[:, c, 0].reshape(rows, width) for c in range(CORE)]
    full_cot = [inputs[:, c, 1].reshape(rows, width) for c in range(CORE)]
    terms = jnp.stack(
        [
            product(full_in[0], expand[0], ((1,), (0,)))
            + product(full_in[1], expand[1], ((1,), (0,))),
            product(full_cot[0], reduce[0], ((1,), (1,)))
            + product(full_cot[1], reduce[1], ((1,), (1,))),
        ]
    )
    share = rows // Y
    terms = terms.reshape(2, Y, share, hidden).transpose(1, 0, 2, 3)
    preact, act_grad = jnp.sum(exchange(terms, "y"), axis=0)
    act_cdf = 0.5 * (1.0 + jax.scipy.special.erf(preact / math.sqrt(2.0)))
    activated = preact * act_cdf
    pre_grad = act_grad * (
        act_cdf + preact * jnp.exp(-0.5 * preact * preact) / math.sqrt(2.0 * math.pi)
    )
    both = exchange(copies(jnp.stack([activated, pre_grad]), Y), "y")
    full_active, full_pregrad = (both[:, k].reshape(rows, hidden) for k in range(2))

    outs = jnp.stack(
        [
            jnp.stack(
                [
                    product(full_active, reduce[c], ((1,), (0,))),
                    product(full_pregrad, expand[c], ((1,), (1,))),
                ]
            )
            for c in range(CORE)
        ]
    )
    outs = outs.reshape(CORE, 2, N_NEAR, N_FAR * part, width).transpose(2, 0, 1, 3, 4)
    outs, full_active, full_pregrad = lax.optimization_barrier((outs, full_active, full_pregrad))
    near = jnp.sum(exchange(outs, CELL, BLOCKS), axis=0)
    near = near.reshape(CORE, 2, N_FAR, part, width).transpose(2, 0, 1, 3, 4)
    last = exchange(near.reshape(N_FAR * CORE, 2, part, width), FAR)
    last = jnp.sum(last.reshape(N_FAR, CORE, 2, part, width), axis=0)
    mlp_output, patch_grad = (last[:, k].reshape(tokens, width) for k in range(2))

    grads = [
        (
            product(full_in[c], full_pregrad, ((0,), (0,))),
            product(full_active, full_cot[c], ((0,), (0,))),
        )
        for c in range(CORE)
    ]
    own, away = zip(*[in_order(a, b) for a, b in zip(*grads)])
    away = swap_cores(jnp.stack(away))
    return mlp_output, patch_grad, own[0] + away[0], own[1] + away[1]


def solution(mesh):
    fine = Mesh(
        mesh.devices.reshape(Y, CORE, ZH, ZL, XH, XL), ("y", "core", "zh", "zl", "xh", "xl")
    )
    row, col = ("y", "core"), ("zh", "zl", "xh", "xl")
    placed = (P(col, row), P(col, row), P(row, col), P(col, row))
    return jax.shard_map(
        shards, mesh=fine, in_specs=placed, out_specs=placed, check_vma=False
    )
```

```python
import math

import jax
import jax.numpy as jnp
from jax import lax
from jax.sharding import Mesh, PartitionSpec as P

precise = lax.Precision.HIGH
Y, CORE, ZH, ZL, XH, XL = 8, 2, 4, 2, 2, 2
N_FAR, N_NEAR, QUAD = ZH * XH, ZL * XL, Y // 2
Z, X = ZH * ZL, XH * XL
CELL = ("core", "zh", "zl", "xh", "xl")
ALL = ("y",) + CELL


def pair_of(c, k, parity):
    return 2 * k + (parity + c) % 2 + c


BLOCKS = [
    [
        (c * Z + pair_of(c, k, (p + c) % 2) % Z) * X + pair_of(c, j, q) % X
        for p in range(2)
        for q in range(2)
    ]
    for c in range(CORE)
    for k in range(ZH)
    for j in range(XH)
]
FAR = [
    [
        (((pair_of(c, k, p) % Y) * CORE + c) * Z + 2 * zh + zl) * X + 2 * xh + xl
        for zh in range(ZH)
        for xh in range(XH)
        for p in range(2)
    ]
    for c in range(CORE)
    for k in range(QUAD)
    for zl in range(ZL)
    for xl in range(XL)
]
PARTNERS = [
    ((pair_of(c, k, p) % Y) * CORE + c, (pair_of(c, k, 1 - p) % Y) * CORE + c)
    for c in range(CORE)
    for k in range(QUAD)
    for p in range(2)
]
QUADS = [list(range(p, Y, 2)) for p in range(2)]


def product(left, right, dims):
    return lax.dot_general(
        left, right, (dims, ((), ())), precision=precise, preferred_element_type=jnp.float32
    )


def swap_cores(block):
    return lax.ppermute(block, "core", [(0, 1), (1, 0)])


def swap_pair(block):
    return lax.ppermute(block, ("y", "core"), PARTNERS)


def exchange(blocks, axis, groups):
    return lax.all_to_all(
        blocks, axis, split_axis=0, concat_axis=0, tiled=True, axis_index_groups=groups
    )


def copies(block, count):
    return jnp.broadcast_to(block[None], (count, *block.shape))


def shards(patches, cotangent, expand_weight, reduce_weight):
    odd = lax.axis_index("y") % 2
    tokens, width = patches.shape
    hidden = expand_weight.shape[1]
    part = tokens // 2
    rows = N_FAR * part

    def own_first(block):
        return jnp.where(odd == 0, block, block[::-1])

    mine = jnp.stack([patches.reshape(2, part, width), cotangent.reshape(2, part, width)], axis=1)
    far = exchange(copies(mine, N_FAR).reshape(2 * N_FAR, 2, part, width), ALL, FAR)
    far = far.reshape(N_FAR, 2, 2, part, width).transpose(1, 2, 0, 3, 4)
    far = own_first(far).reshape(2, 2, rows, width)
    far, other_expand = lax.optimization_barrier((far, swap_pair(expand_weight)))
    inputs = exchange(copies(far, N_NEAR), CELL, BLOCKS)

    expand = (expand_weight, other_expand)
    reduce = (reduce_weight, swap_pair(reduce_weight))

    half = N_NEAR // 2 * rows

    def terms(block):
        def take(pair, array):
            return block[:, pair, array].reshape(half, width)

        return jnp.stack(
            [
                product(take(0, 0), expand[0], ((1,), (0,)))
                + product(take(1, 0), expand[1], ((1,), (0,))),
                product(take(0, 1), reduce[0], ((1,), (1,)))
                + product(take(1, 1), reduce[1], ((1,), (1,))),
            ]
        )

    away = swap_cores(terms(inputs[N_NEAR // 2 :]))
    share = half // QUAD
    summed = (terms(inputs[: N_NEAR // 2]) + away).reshape(2, QUAD, share, hidden)
    preact, act_grad = jnp.sum(exchange(summed.transpose(1, 0, 2, 3), "y", QUADS), axis=0)
    act_cdf = 0.5 * (1.0 + jax.scipy.special.erf(preact / math.sqrt(2.0)))
    activated = preact * act_cdf
    pre_grad = act_grad * (
        act_cdf + preact * jnp.exp(-0.5 * preact * preact) / math.sqrt(2.0 * math.pi)
    )
    own = exchange(copies(jnp.stack([activated, pre_grad]), QUAD), "y", QUADS)
    other = swap_cores(own)

    def results(both):
        active, pregrad = (both[:, k].reshape(half, hidden) for k in range(2))
        return jnp.stack(
            [
                jnp.stack(
                    [
                        product(active, reduce[p], ((1,), (0,))),
                        product(pregrad, expand[p], ((1,), (1,))),
                    ]
                ).reshape(2, N_NEAR // 2, rows, width)
                for p in range(2)
            ]
        )

    outs = jnp.concatenate([results(own), results(other)], axis=2)
    outs = outs.transpose(2, 0, 1, 3, 4)
    outs, own, other = lax.optimization_barrier((outs, own, other))
    near = jnp.sum(exchange(outs, CELL, BLOCKS), axis=0)
    near = own_first(near).reshape(2, 2, N_FAR, part, width).transpose(2, 0, 1, 3, 4)

    flat = [
        jnp.concatenate([own[:, k].reshape(half, hidden), other[:, k].reshape(half, hidden)])
        for k in range(2)
    ]
    grads = [
        jnp.stack(
            [
                product(inputs[:, p, 0].reshape(2 * half, width), flat[1], ((0,), (0,))),
                product(flat[0], inputs[:, p, 1].reshape(2 * half, width), ((0,), (0,))),
            ]
        )
        for p in range(2)
    ]
    away = swap_pair(grads[1])
    last = exchange(near.reshape(2 * N_FAR, 2, part, width), ALL, FAR)
    last = jnp.sum(last.reshape(N_FAR, 2, 2, part, width), axis=0)
    mlp_output, patch_grad = (last[:, k].reshape(tokens, width) for k in range(2))
    return mlp_output, patch_grad, grads[0][0] + away[0], grads[0][1] + away[1]


def solution(mesh):
    fine = Mesh(mesh.devices.reshape(Y, CORE, ZH, ZL, XH, XL), ALL)
    row, col = ("y", "core"), ("zh", "zl", "xh", "xl")
    placed = (P(col, row), P(col, row), P(row, col), P(col, row))
    return jax.shard_map(
        shards, mesh=fine, in_specs=placed, out_specs=placed, check_vma=False
    )
```

```python
import functools
import math

import jax
import jax.numpy as jnp
from jax import lax
from jax.experimental import pallas as pl
from jax.experimental.pallas import tpu as pltpu
from jax.sharding import Mesh, PartitionSpec as P

precise = lax.Precision.HIGH
Y, CORE, ZH, ZL, XH, XL = 8, 2, 4, 2, 2, 2
N_FAR, N_NEAR, QUAD = ZH * XH, ZL * XL, Y // 2
Z, X = ZH * ZL, XH * XL
CELL = ("core", "zh", "zl", "xh", "xl")
ALL = ("y",) + CELL


def pair_of(c, k, parity):
    return 2 * k + (parity + c) % 2 + c


BLOCKS = [
    [
        (c * Z + pair_of(c, k, (p + c) % 2) % Z) * X + pair_of(c, j, q) % X
        for p in range(2)
        for q in range(2)
    ]
    for c in range(CORE)
    for k in range(ZH)
    for j in range(XH)
]
FAR = [
    [
        (((pair_of(c, k, p) % Y) * CORE + c) * Z + 2 * zh + zl) * X + 2 * xh + xl
        for zh in range(ZH)
        for xh in range(XH)
        for p in range(2)
    ]
    for c in range(CORE)
    for k in range(QUAD)
    for zl in range(ZL)
    for xl in range(XL)
]
PARTNERS = [
    ((pair_of(c, k, p) % Y) * CORE + c, (pair_of(c, k, 1 - p) % Y) * CORE + c)
    for c in range(CORE)
    for k in range(QUAD)
    for p in range(2)
]
QUADS = [list(range(p, Y, 2)) for p in range(2)]


def product(left, right, dims):
    return lax.dot_general(
        left, right, (dims, ((), ())), precision=precise, preferred_element_type=jnp.float32
    )


def halves(block):
    high = block.astype(jnp.bfloat16)
    return high, (block - high.astype(jnp.float32)).astype(jnp.bfloat16)


def product_of_halves(left, right, flipped):
    dims = (((1,), (1 if flipped else 0,)), ((), ()))

    def dot(a, b):
        return lax.dot_general(a, b, dims, preferred_element_type=jnp.float32)

    return dot(left[0], right[0]) + (dot(left[0], right[1]) + dot(left[1], right[0]))


def terms_kernel(first, share, inputs, expand, expand_far, reduce, reduce_far, out):
    weights = ((expand, expand_far), (reduce, reduce_far))
    for array in range(2):
        total = None
        for pair in range(2):
            block = jnp.concatenate([inputs[first + n, pair, array] for n in range(2)], axis=0)
            term = product_of_halves(
                halves(block), halves(weights[array][pair][...]), array == 1
            )
            total = term if total is None else total + term
        for q in range(QUAD):
            out[q, array] = total[q * share : (q + 1) * share]


def results_kernel(earlier, both, expand, expand_far, reduce, reduce_far, out):
    at = 0
    if earlier is not None:
        at = earlier.shape[0]
        out[:at] = earlier[...]
    rows = out.shape[3]
    weights = ((reduce, reduce_far), (expand, expand_far))
    for array in range(2):
        block = halves(jnp.concatenate([both[q, array] for q in range(QUAD)], axis=0))
        for pair in range(2):
            term = product_of_halves(block, halves(weights[array][pair][...]), array == 1)
            for n in range(2):
                out[at + n, pair, array] = term[n * rows : (n + 1) * rows]


def send_kernel(patches, cotangent, out):
    part = out.shape[3]
    for p in range(2):
        for array, source in enumerate((patches, cotangent)):
            block = source[p * part : (p + 1) * part]
            for m in range(N_FAR):
                out[m, p, array] = block


def spread_kernel(odd, far, out):
    part = far.shape[3]
    for p in range(2):
        source = jnp.bitwise_xor(odd[0], p)
        for array in range(2):
            for m in range(N_FAR):
                block = far[m, source, array]
                for n in range(N_NEAR):
                    out[n, p, array, m * part : (m + 1) * part] = block


def fold_kernel(odd, near, out):
    part = out.shape[3]
    for p in range(2):
        target = jnp.bitwise_xor(odd[0], p)
        for array in range(2):
            total = (near[0, p, array] + near[1, p, array]) + (
                near[2, p, array] + near[3, p, array]
            )
            for m in range(N_FAR):
                out[m, target, array] = total[m * part : (m + 1) * part]


def local_call(kernel, shape, flops, *operands):
    bytes_accessed = 4 * (math.prod(shape) + sum(v.size for v in operands))
    return pl.pallas_call(
        kernel,
        out_shape=jax.ShapeDtypeStruct(shape, jnp.float32),
        in_specs=[
            pl.BlockSpec(memory_space=pltpu.SMEM if v.dtype == jnp.int32 else pltpu.VMEM)
            for v in operands
        ],
        out_specs=pl.BlockSpec(memory_space=pltpu.VMEM),
        compiler_params=pltpu.CompilerParams(vmem_limit_bytes=8 * 2**20),
        cost_estimate=pl.CostEstimate(
            flops=flops, bytes_accessed=bytes_accessed, transcendentals=0
        ),
    )(*operands)


def swap_cores(block):
    return lax.ppermute(block, "core", [(0, 1), (1, 0)])


def swap_pair(block):
    return lax.ppermute(block, ("y", "core"), PARTNERS)


def exchange(blocks, axis, groups):
    return lax.all_to_all(
        blocks, axis, split_axis=0, concat_axis=0, tiled=True, axis_index_groups=groups
    )


def copies(block, count):
    return jnp.broadcast_to(block[None], (count, *block.shape))


def shards(patches, cotangent, expand_weight, reduce_weight):
    odd = (lax.axis_index("y") % 2).reshape(1)
    tokens, width = patches.shape
    hidden = expand_weight.shape[1]
    part = tokens // 2
    rows = N_FAR * part

    mine = local_call(send_kernel, (N_FAR, 2, 2, part, width), 0, patches, cotangent)
    far = exchange(mine.reshape(2 * N_FAR, 2, part, width), ALL, FAR)
    far = far.reshape(N_FAR, 2, 2, part, width)
    far, other_expand = lax.optimization_barrier((far, swap_pair(expand_weight)))
    inputs = local_call(spread_kernel, (N_NEAR, 2, 2, rows, width), 0, odd, far)
    inputs = exchange(inputs, CELL, BLOCKS)

    expand = (expand_weight, other_expand)
    reduce = (reduce_weight, swap_pair(reduce_weight))

    half = N_NEAR // 2 * rows
    share = half // QUAD
    flops = 3 * 2 * 4 * half * width * hidden
    weights = (*expand, *reduce)

    def terms(first):
        return local_call(
            functools.partial(terms_kernel, first, share),
            (QUAD, 2, share, hidden),
            flops,
            inputs,
            *weights,
        )

    summed = swap_cores(terms(N_NEAR // 2))
    summed = terms(0) + summed
    preact, act_grad = jnp.sum(exchange(summed, "y", QUADS), axis=0)
    act_cdf = 0.5 * (1.0 + jax.scipy.special.erf(preact / math.sqrt(2.0)))
    activated = preact * act_cdf
    pre_grad = act_grad * (
        act_cdf + preact * jnp.exp(-0.5 * preact * preact) / math.sqrt(2.0 * math.pi)
    )
    own = exchange(copies(jnp.stack([activated, pre_grad]), QUAD), "y", QUADS)
    other = swap_cores(own)

    tail = (2, 2, rows, width)
    outs = local_call(
        functools.partial(results_kernel, None), (N_NEAR // 2, *tail), flops, own, *weights
    )
    outs = local_call(results_kernel, (N_NEAR, *tail), flops, outs, other, *weights)
    outs, own, other = lax.optimization_barrier((outs, own, other))
    near = exchange(outs, CELL, BLOCKS)
    near = local_call(fold_kernel, (N_FAR, 2, 2, part, width), near.size, odd, near)

    flat = [
        jnp.concatenate([own[:, k].reshape(half, hidden), other[:, k].reshape(half, hidden)])
        for k in range(2)
    ]
    grads = [
        jnp.stack(
            [
                product(inputs[:, p, 0].reshape(2 * half, width), flat[1], ((0,), (0,))),
                product(flat[0], inputs[:, p, 1].reshape(2 * half, width), ((0,), (0,))),
            ]
        )
        for p in range(2)
    ]
    away = swap_pair(grads[1])
    last = exchange(near.reshape(2 * N_FAR, 2, part, width), ALL, FAR)
    last = jnp.sum(last.reshape(N_FAR, 2, 2, part, width), axis=0)
    mlp_output, patch_grad = (last[:, k].reshape(tokens, width) for k in range(2))
    return mlp_output, patch_grad, grads[0][0] + away[0], grads[0][1] + away[1]


def solution(mesh):
    fine = Mesh(mesh.devices.reshape(Y, CORE, ZH, ZL, XH, XL), ALL)
    row, col = ("y", "core"), ("zh", "zl", "xh", "xl")
    placed = (P(col, row), P(col, row), P(row, col), P(col, row))
    return jax.shard_map(
        shards, mesh=fine, in_specs=placed, out_specs=placed, check_vma=False
    )
```

```python
import functools
import math

import jax
import jax.numpy as jnp
from jax import lax
from jax.experimental import pallas as pl
from jax.experimental.pallas import tpu as pltpu
from jax.sharding import Mesh, PartitionSpec as P

precise = lax.Precision.HIGH
Y, CORE, ZH, ZL, XH, XL = 8, 2, 4, 2, 2, 2
N_FAR, N_NEAR, QUAD = ZH * XH, ZL * XL, Y // 2
Z, X = ZH * ZL, XH * XL
CELL = ("core", "zh", "zl", "xh", "xl")
ALL = ("y",) + CELL


def pair_of(c, k, parity):
    return 2 * k + (parity + c) % 2 + c


BLOCKS = [
    [
        (c * Z + pair_of(c, k, (p + c) % 2) % Z) * X + pair_of(c, j, q) % X
        for p in range(2)
        for q in range(2)
    ]
    for c in range(CORE)
    for k in range(ZH)
    for j in range(XH)
]
FAR = [
    [
        (((pair_of(c, k, p) % Y) * CORE + c) * Z + 2 * zh + zl) * X + 2 * xh + xl
        for zh in range(ZH)
        for xh in range(XH)
        for p in range(2)
    ]
    for c in range(CORE)
    for k in range(QUAD)
    for zl in range(ZL)
    for xl in range(XL)
]
PARTNERS = [
    ((pair_of(c, k, p) % Y) * CORE + c, (pair_of(c, k, 1 - p) % Y) * CORE + c)
    for c in range(CORE)
    for k in range(QUAD)
    for p in range(2)
]
QUADS = [list(range(p, Y, 2)) for p in range(2)]


def product(left, right, dims):
    return lax.dot_general(
        left, right, (dims, ((), ())), precision=precise, preferred_element_type=jnp.float32
    )


def halves(block):
    high = block.astype(jnp.bfloat16)
    return high, (block - high.astype(jnp.float32)).astype(jnp.bfloat16)


def product_of_halves(left, right, flipped):
    dims = (((1,), (1 if flipped else 0,)), ((), ()))

    def dot(a, b):
        return lax.dot_general(a, b, dims, preferred_element_type=jnp.float32)

    return dot(left[0], right[0]) + (dot(left[0], right[1]) + dot(left[1], right[0]))


def terms_kernel(first, share, inputs, expand, expand_far, reduce, reduce_far, out):
    weights = ((expand, expand_far), (reduce, reduce_far))
    for array in range(2):
        total = None
        for pair in range(2):
            block = jnp.concatenate([inputs[first + n, pair, array] for n in range(2)], axis=0)
            term = product_of_halves(
                halves(block), halves(weights[array][pair][...]), array == 1
            )
            total = term if total is None else total + term
        for q in range(QUAD):
            out[q, array] = total[q * share : (q + 1) * share]


def results_kernel(earlier, both, expand, expand_far, reduce, reduce_far, out):
    at = 0
    if earlier is not None:
        at = earlier.shape[0]
        out[:at] = earlier[...]
    rows = out.shape[3]
    weights = ((reduce, reduce_far), (expand, expand_far))
    for array in range(2):
        block = halves(jnp.concatenate([both[q, array] for q in range(QUAD)], axis=0))
        for pair in range(2):
            term = product_of_halves(block, halves(weights[array][pair][...]), array == 1)
            for n in range(2):
                out[at + n, pair, array] = term[n * rows : (n + 1) * rows]


def spread_kernel(odd, far, out):
    part = far.shape[3]
    for p in range(2):
        source = jnp.bitwise_xor(odd[0], p)
        for array in range(2):
            for m in range(N_FAR):
                block = far[m, source, array]
                for n in range(N_NEAR):
                    out[n, p, array, m * part : (m + 1) * part] = block


def fold_kernel(odd, near, out):
    part = out.shape[3]
    for p in range(2):
        target = jnp.bitwise_xor(odd[0], p)
        for array in range(2):
            total = (near[0, p, array] + near[1, p, array]) + (
                near[2, p, array] + near[3, p, array]
            )
            for m in range(N_FAR):
                out[m, target, array] = total[m * part : (m + 1) * part]


def local_call(kernel, shape, flops, *operands):
    bytes_accessed = 4 * (math.prod(shape) + sum(v.size for v in operands))
    return pl.pallas_call(
        kernel,
        out_shape=jax.ShapeDtypeStruct(shape, jnp.float32),
        in_specs=[
            pl.BlockSpec(memory_space=pltpu.SMEM if v.dtype == jnp.int32 else pltpu.VMEM)
            for v in operands
        ],
        out_specs=pl.BlockSpec(memory_space=pltpu.VMEM),
        compiler_params=pltpu.CompilerParams(vmem_limit_bytes=8 * 2**20),
        cost_estimate=pl.CostEstimate(
            flops=flops, bytes_accessed=bytes_accessed, transcendentals=0
        ),
    )(*operands)


def swap_cores(block):
    return lax.ppermute(block, "core", [(0, 1), (1, 0)])


def swap_pair(block):
    return lax.ppermute(block, ("y", "core"), PARTNERS)


def exchange(blocks, axis, groups):
    return lax.all_to_all(
        blocks, axis, split_axis=0, concat_axis=0, tiled=True, axis_index_groups=groups
    )


def copies(block, count):
    return jnp.broadcast_to(block[None], (count, *block.shape))


def shards(patches, cotangent, expand_weight, reduce_weight):
    odd = (lax.axis_index("y") % 2).reshape(1)
    tokens, width = patches.shape
    hidden = expand_weight.shape[1]
    part = tokens // 2
    rows = N_FAR * part

    mine = jnp.stack([patches.reshape(2, part, width), cotangent.reshape(2, part, width)], axis=1)
    far = exchange(copies(mine, N_FAR).reshape(2 * N_FAR, 2, part, width), ALL, FAR)
    far = far.reshape(N_FAR, 2, 2, part, width)
    far, other_expand = lax.optimization_barrier((far, swap_pair(expand_weight)))
    inputs = local_call(spread_kernel, (N_NEAR, 2, 2, rows, width), 0, odd, far)
    inputs = exchange(inputs, CELL, BLOCKS)

    expand = (expand_weight, other_expand)
    reduce = (reduce_weight, swap_pair(reduce_weight))

    half = N_NEAR // 2 * rows
    share = half // QUAD
    flops = 3 * 2 * 4 * half * width * hidden
    weights = (*expand, *reduce)

    def terms(first):
        return local_call(
            functools.partial(terms_kernel, first, share),
            (QUAD, 2, share, hidden),
            flops,
            inputs,
            *weights,
        )

    summed = swap_cores(terms(N_NEAR // 2))
    summed = terms(0) + summed
    preact, act_grad = jnp.sum(exchange(summed, "y", QUADS), axis=0)
    act_cdf = 0.5 * (1.0 + jax.scipy.special.erf(preact / math.sqrt(2.0)))
    activated = preact * act_cdf
    pre_grad = act_grad * (
        act_cdf + preact * jnp.exp(-0.5 * preact * preact) / math.sqrt(2.0 * math.pi)
    )
    own = exchange(copies(jnp.stack([activated, pre_grad]), QUAD), "y", QUADS)
    other = swap_cores(own)

    tail = (2, 2, rows, width)
    outs = local_call(
        functools.partial(results_kernel, None), (N_NEAR // 2, *tail), flops, own, *weights
    )
    outs = local_call(results_kernel, (N_NEAR, *tail), flops, outs, other, *weights)
    near = exchange(outs, CELL, BLOCKS)
    near = local_call(fold_kernel, (N_FAR, 2, 2, part, width), near.size, odd, near)

    flat = [
        jnp.concatenate([own[:, k].reshape(half, hidden), other[:, k].reshape(half, hidden)])
        for k in range(2)
    ]
    grads = [
        jnp.stack(
            [
                product(inputs[:, p, 0].reshape(2 * half, width), flat[1], ((0,), (0,))),
                product(flat[0], inputs[:, p, 1].reshape(2 * half, width), ((0,), (0,))),
            ]
        )
        for p in range(2)
    ]
    away = swap_pair(grads[1])
    last = exchange(near.reshape(2 * N_FAR, 2, part, width), ALL, FAR)
    last = jnp.sum(last.reshape(N_FAR, 2, 2, part, width), axis=0)
    mlp_output, patch_grad = (last[:, k].reshape(tokens, width) for k in range(2))
    return mlp_output, patch_grad, grads[0][0] + away[0], grads[0][1] + away[1]


def solution(mesh):
    fine = Mesh(mesh.devices.reshape(Y, CORE, ZH, ZL, XH, XL), ALL)
    row, col = ("y", "core"), ("zh", "zl", "xh", "xl")
    placed = (P(col, row), P(col, row), P(row, col), P(col, row))
    return jax.shard_map(
        shards, mesh=fine, in_specs=placed, out_specs=placed, check_vma=False
    )
```

```python
import functools
import math

import jax
import jax.numpy as jnp
from jax import lax
from jax.experimental import pallas as pl
from jax.experimental.pallas import tpu as pltpu
from jax.sharding import Mesh, PartitionSpec as P

precise = lax.Precision.HIGH
Y, CORE, ZH, ZL, XH, XL = 8, 2, 4, 2, 2, 2
N_FAR, N_NEAR, QUAD = ZH * XH, ZL * XL, Y // 2
Z, X = ZH * ZL, XH * XL
CELL = ("core", "zh", "zl", "xh", "xl")
ALL = ("y",) + CELL


def pair_of(c, k, parity):
    return 2 * k + (parity + c) % 2 + c


BLOCKS = [
    [
        (c * Z + pair_of(c, k, (p + c) % 2) % Z) * X + pair_of(c, j, q) % X
        for p in range(2)
        for q in range(2)
    ]
    for c in range(CORE)
    for k in range(ZH)
    for j in range(XH)
]
FAR = [
    [
        (((pair_of(c, k, p) % Y) * CORE + c) * Z + 2 * zh + zl) * X + 2 * xh + xl
        for zh in range(ZH)
        for xh in range(XH)
        for p in range(2)
    ]
    for c in range(CORE)
    for k in range(QUAD)
    for zl in range(ZL)
    for xl in range(XL)
]
PARTNERS = [
    ((pair_of(c, k, p) % Y) * CORE + c, (pair_of(c, k, 1 - p) % Y) * CORE + c)
    for c in range(CORE)
    for k in range(QUAD)
    for p in range(2)
]
QUADS = [list(range(p, Y, 2)) for p in range(2)]


def product(left, right, dims):
    return lax.dot_general(
        left, right, (dims, ((), ())), precision=precise, preferred_element_type=jnp.float32
    )


def halves(block):
    high = block.astype(jnp.bfloat16)
    return high, (block - high.astype(jnp.float32)).astype(jnp.bfloat16)


def product_of_halves(left, right, flipped):
    dims = (((1,), (1 if flipped else 0,)), ((), ()))

    def dot(a, b):
        return lax.dot_general(a, b, dims, preferred_element_type=jnp.float32)

    return dot(left[0], right[0]) + (dot(left[0], right[1]) + dot(left[1], right[0]))


def terms_kernel(first, share, inputs, expand, expand_far, reduces, out):
    weights = ((expand, expand_far), (reduces.at[0], reduces.at[1]))
    for array in range(2):
        total = None
        for pair in range(2):
            block = jnp.concatenate([inputs[first + n, pair, array] for n in range(2)], axis=0)
            term = product_of_halves(
                halves(block), halves(weights[array][pair][...]), array == 1
            )
            total = term if total is None else total + term
        for q in range(QUAD):
            out[q, array] = total[q * share : (q + 1) * share]


def results_kernel(earlier, both, expand, expand_far, reduces, out):
    at = 0
    if earlier is not None:
        at = earlier.shape[0]
        out[:at] = earlier[...]
    rows = out.shape[3]
    weights = ((reduces.at[0], reduces.at[1]), (expand, expand_far))
    for array in range(2):
        block = halves(jnp.concatenate([both[q, array] for q in range(QUAD)], axis=0))
        for pair in range(2):
            term = product_of_halves(block, halves(weights[array][pair][...]), array == 1)
            for n in range(2):
                out[at + n, pair, array] = term[n * rows : (n + 1) * rows]


def spread_kernel(odd, far, out):
    part = far.shape[3]
    for p in range(2):
        source = jnp.bitwise_xor(odd[0], p)
        for array in range(2):
            for m in range(N_FAR):
                block = far[m, source, array]
                for n in range(N_NEAR):
                    out[n, p, array, m * part : (m + 1) * part] = block


def fold_kernel(odd, near, out):
    part = out.shape[3]
    for p in range(2):
        target = jnp.bitwise_xor(odd[0], p)
        for array in range(2):
            total = (near[0, p, array] + near[1, p, array]) + (
                near[2, p, array] + near[3, p, array]
            )
            for m in range(N_FAR):
                out[m, target, array] = total[m * part : (m + 1) * part]


def local_call(kernel, shape, flops, *operands):
    bytes_accessed = 4 * (math.prod(shape) + sum(v.size for v in operands))
    return pl.pallas_call(
        kernel,
        out_shape=jax.ShapeDtypeStruct(shape, jnp.float32),
        in_specs=[
            pl.BlockSpec(memory_space=pltpu.SMEM if v.dtype == jnp.int32 else pltpu.VMEM)
            for v in operands
        ],
        out_specs=pl.BlockSpec(memory_space=pltpu.VMEM),
        compiler_params=pltpu.CompilerParams(vmem_limit_bytes=8 * 2**20),
        cost_estimate=pl.CostEstimate(
            flops=flops, bytes_accessed=bytes_accessed, transcendentals=0
        ),
    )(*operands)


def swap_cores(block):
    return lax.ppermute(block, "core", [(0, 1), (1, 0)])


def swap_pair(block):
    return lax.ppermute(block, ("y", "core"), PARTNERS)


def exchange(blocks, axis, groups):
    return lax.all_to_all(
        blocks, axis, split_axis=0, concat_axis=0, tiled=True, axis_index_groups=groups
    )


def copies(block, count):
    return jnp.broadcast_to(block[None], (count, *block.shape))


def shards(patches, cotangent, expand_weight, reduce_weight):
    odd = (lax.axis_index("y") % 2).reshape(1)
    tokens, width = patches.shape
    hidden = expand_weight.shape[1]
    part = tokens // 2
    rows = N_FAR * part

    mine = jnp.stack([patches.reshape(2, part, width), cotangent.reshape(2, part, width)], axis=1)
    far = exchange(copies(mine, N_FAR).reshape(2 * N_FAR, 2, part, width), ALL, FAR)
    far = far.reshape(N_FAR, 2, 2, part, width)
    far, other_expand = lax.optimization_barrier((far, swap_pair(expand_weight)))
    inputs = local_call(spread_kernel, (N_NEAR, 2, 2, rows, width), 0, odd, far)
    inputs = exchange(inputs, CELL, BLOCKS)

    expand = (expand_weight, other_expand)
    reduces = jnp.stack([reduce_weight, swap_pair(reduce_weight)])

    half = N_NEAR // 2 * rows
    share = half // QUAD
    flops = 3 * 2 * 4 * half * width * hidden
    weights = (*expand, reduces)

    def terms(first):
        return local_call(
            functools.partial(terms_kernel, first, share),
            (QUAD, 2, share, hidden),
            flops,
            inputs,
            *weights,
        )

    summed = swap_cores(terms(N_NEAR // 2))
    summed = terms(0) + summed
    preact, act_grad = jnp.sum(exchange(summed, "y", QUADS), axis=0)
    act_cdf = 0.5 * (1.0 + jax.scipy.special.erf(preact / math.sqrt(2.0)))
    activated = preact * act_cdf
    pre_grad = act_grad * (
        act_cdf + preact * jnp.exp(-0.5 * preact * preact) / math.sqrt(2.0 * math.pi)
    )
    own = exchange(copies(jnp.stack([activated, pre_grad]), QUAD), "y", QUADS)
    other = swap_cores(own)

    tail = (2, 2, rows, width)
    outs = local_call(
        functools.partial(results_kernel, None), (N_NEAR // 2, *tail), flops, own, *weights
    )
    outs = local_call(results_kernel, (N_NEAR, *tail), flops, outs, other, *weights)
    near = exchange(outs, CELL, BLOCKS)
    near = local_call(fold_kernel, (N_FAR, 2, 2, part, width), near.size, odd, near)

    flat = [
        jnp.concatenate([own[:, k].reshape(half, hidden), other[:, k].reshape(half, hidden)])
        for k in range(2)
    ]
    grads = [
        jnp.stack(
            [
                product(inputs[:, p, 0].reshape(2 * half, width), flat[1], ((0,), (0,))),
                product(flat[0], inputs[:, p, 1].reshape(2 * half, width), ((0,), (0,))),
            ]
        )
        for p in range(2)
    ]
    away = swap_pair(grads[1])
    last = exchange(near.reshape(2 * N_FAR, 2, part, width), ALL, FAR)
    last = jnp.sum(last.reshape(N_FAR, 2, 2, part, width), axis=0)
    mlp_output, patch_grad = (last[:, k].reshape(tokens, width) for k in range(2))
    return mlp_output, patch_grad, grads[0][0] + away[0], grads[0][1] + away[1]


def solution(mesh):
    fine = Mesh(mesh.devices.reshape(Y, CORE, ZH, ZL, XH, XL), ALL)
    row, col = ("y", "core"), ("zh", "zl", "xh", "xl")
    placed = (P(col, row), P(col, row), P(row, col), P(col, row))
    return jax.shard_map(
        shards, mesh=fine, in_specs=placed, out_specs=placed, check_vma=False
    )
```

```python
import functools
import math

import jax
import jax.numpy as jnp
from jax import lax
from jax.experimental import pallas as pl
from jax.experimental.pallas import tpu as pltpu
from jax.sharding import Mesh, PartitionSpec as P

precise = lax.Precision.HIGH
Y, CORE, ZH, ZL, XH, XL = 8, 2, 4, 2, 2, 2
N_FAR, N_NEAR, QUAD = ZH * XH, ZL * XL, Y // 2
Z, X = ZH * ZL, XH * XL
CELL = ("core", "zh", "zl", "xh", "xl")
ALL = ("y",) + CELL


def pair_of(c, k, parity):
    return 2 * k + (parity + c) % 2 + c


BLOCKS = [
    [
        (c * Z + pair_of(c, k, (p + c) % 2) % Z) * X + pair_of(c, j, q) % X
        for p in range(2)
        for q in range(2)
    ]
    for c in range(CORE)
    for k in range(ZH)
    for j in range(XH)
]
FAR = [
    [
        (((pair_of(c, k, p) % Y) * CORE + c) * Z + 2 * zh + zl) * X + 2 * xh + xl
        for zh in range(ZH)
        for xh in range(XH)
        for p in range(2)
    ]
    for c in range(CORE)
    for k in range(QUAD)
    for zl in range(ZL)
    for xl in range(XL)
]
PARTNERS = [
    ((pair_of(c, k, p) % Y) * CORE + c, (pair_of(c, k, 1 - p) % Y) * CORE + c)
    for c in range(CORE)
    for k in range(QUAD)
    for p in range(2)
]
QUADS = [list(range(p, Y, 2)) for p in range(2)]


def product(left, right, dims):
    return lax.dot_general(
        left, right, (dims, ((), ())), precision=precise, preferred_element_type=jnp.float32
    )


def halves(block):
    high = block.astype(jnp.bfloat16)
    return high, (block - high.astype(jnp.float32)).astype(jnp.bfloat16)


def product_of_halves(left, right, flipped):
    dims = (((1,), (1 if flipped else 0,)), ((), ()))

    def dot(a, b):
        return lax.dot_general(a, b, dims, preferred_element_type=jnp.float32)

    return dot(left[0], right[0]) + (dot(left[0], right[1]) + dot(left[1], right[0]))


def terms_kernel(first, share, inputs, expand, expand_far, reduce, reduce_far, out):
    weights = ((expand, expand_far), (reduce, reduce_far))
    for array in range(2):
        total = None
        for pair in range(2):
            block = jnp.concatenate([inputs[first + n, pair, array] for n in range(2)], axis=0)
            term = product_of_halves(
                halves(block), halves(weights[array][pair][...]), array == 1
            )
            total = term if total is None else total + term
        for q in range(QUAD):
            out[q, array] = total[q * share : (q + 1) * share]


def results_kernel(earlier, both, expand, expand_far, reduce, reduce_far, out):
    at = 0
    if earlier is not None:
        at = earlier.shape[0]
        out[:at] = earlier[...]
    rows = out.shape[3]
    weights = ((reduce, reduce_far), (expand, expand_far))
    for array in range(2):
        block = halves(jnp.concatenate([both[q, array] for q in range(QUAD)], axis=0))
        for pair in range(2):
            term = product_of_halves(block, halves(weights[array][pair][...]), array == 1)
            for n in range(2):
                out[at + n, pair, array] = term[n * rows : (n + 1) * rows]


def spread_kernel(odd, far, out):
    part = far.shape[3]
    for p in range(2):
        source = jnp.bitwise_xor(odd[0], p)
        for array in range(2):
            for m in range(N_FAR):
                block = far[m, source, array]
                for n in range(N_NEAR):
                    out[n, p, array, m * part : (m + 1) * part] = block


def fold_kernel(odd, near, out):
    part = out.shape[3]
    for p in range(2):
        target = jnp.bitwise_xor(odd[0], p)
        for array in range(2):
            total = (near[0, p, array] + near[1, p, array]) + (
                near[2, p, array] + near[3, p, array]
            )
            for m in range(N_FAR):
                out[m, target, array] = total[m * part : (m + 1) * part]


def local_call(kernel, shape, flops, *operands):
    bytes_accessed = 4 * (math.prod(shape) + sum(v.size for v in operands))
    return pl.pallas_call(
        kernel,
        out_shape=jax.ShapeDtypeStruct(shape, jnp.float32),
        in_specs=[
            pl.BlockSpec(memory_space=pltpu.SMEM if v.dtype == jnp.int32 else pltpu.VMEM)
            for v in operands
        ],
        out_specs=pl.BlockSpec(memory_space=pltpu.VMEM),
        compiler_params=pltpu.CompilerParams(vmem_limit_bytes=8 * 2**20),
        cost_estimate=pl.CostEstimate(
            flops=flops, bytes_accessed=bytes_accessed, transcendentals=0
        ),
    )(*operands)


def swap_cores(block):
    return lax.ppermute(block, "core", [(0, 1), (1, 0)])


def swap_pair(block):
    return lax.ppermute(block, ("y", "core"), PARTNERS)


def exchange(blocks, axis, groups):
    return lax.all_to_all(
        blocks, axis, split_axis=0, concat_axis=0, tiled=True, axis_index_groups=groups
    )


def copies(block, count):
    return jnp.broadcast_to(block[None], (count, *block.shape))


def shards(patches, cotangent, expand_weight, reduce_weight):
    odd = (lax.axis_index("y") % 2).reshape(1)
    tokens, width = patches.shape
    hidden = expand_weight.shape[1]
    part = tokens // 2
    rows = N_FAR * part

    mine = jnp.stack([patches.reshape(2, part, width), cotangent.reshape(2, part, width)], axis=1)
    far = exchange(copies(mine, N_FAR).reshape(2 * N_FAR, 2, part, width), ALL, FAR)
    far = far.reshape(N_FAR, 2, 2, part, width)
    far, other_expand = lax.optimization_barrier((far, swap_pair(expand_weight)))
    inputs = local_call(spread_kernel, (N_NEAR, 2, 2, rows, width), 0, odd, far)
    inputs = exchange(inputs, CELL, BLOCKS)

    expand = (expand_weight, other_expand)
    reduce = (reduce_weight, swap_pair(reduce_weight))

    half = N_NEAR // 2 * rows
    share = half // QUAD
    flops = 3 * 2 * 4 * half * width * hidden
    weights = (*expand, *reduce)

    def terms(first):
        return local_call(
            functools.partial(terms_kernel, first, share),
            (QUAD, 2, share, hidden),
            flops,
            inputs,
            *weights,
        )

    summed = swap_cores(terms(N_NEAR // 2))
    summed = terms(0) + summed
    preact, act_grad = jnp.sum(exchange(summed, "y", QUADS), axis=0)
    act_cdf = 0.5 * (1.0 + jax.scipy.special.erf(preact / math.sqrt(2.0)))
    activated = preact * act_cdf
    pre_grad = act_grad * (
        act_cdf + preact * jnp.exp(-0.5 * preact * preact) / math.sqrt(2.0 * math.pi)
    )
    own = exchange(copies(jnp.stack([activated, pre_grad]), QUAD), "y", QUADS)
    other = swap_cores(own)

    tail = (2, 2, rows, width)
    outs = jnp.concatenate(
        [
            local_call(
                functools.partial(results_kernel, None),
                (N_NEAR // 2, *tail),
                flops,
                both,
                *weights,
            )
            for both in (own, other)
        ]
    )
    near = exchange(outs, CELL, BLOCKS)
    near = local_call(fold_kernel, (N_FAR, 2, 2, part, width), near.size, odd, near)

    flat = [
        jnp.concatenate([own[:, k].reshape(half, hidden), other[:, k].reshape(half, hidden)])
        for k in range(2)
    ]
    grads = [
        jnp.stack(
            [
                product(inputs[:, p, 0].reshape(2 * half, width), flat[1], ((0,), (0,))),
                product(flat[0], inputs[:, p, 1].reshape(2 * half, width), ((0,), (0,))),
            ]
        )
        for p in range(2)
    ]
    away = swap_pair(grads[1])
    last = exchange(near.reshape(2 * N_FAR, 2, part, width), ALL, FAR)
    last = jnp.sum(last.reshape(N_FAR, 2, 2, part, width), axis=0)
    mlp_output, patch_grad = (last[:, k].reshape(tokens, width) for k in range(2))
    return mlp_output, patch_grad, grads[0][0] + away[0], grads[0][1] + away[1]


def solution(mesh):
    fine = Mesh(mesh.devices.reshape(Y, CORE, ZH, ZL, XH, XL), ALL)
    row, col = ("y", "core"), ("zh", "zl", "xh", "xl")
    placed = (P(col, row), P(col, row), P(row, col), P(col, row))
    return jax.shard_map(
        shards, mesh=fine, in_specs=placed, out_specs=placed, check_vma=False
    )
```
